256 devices in a mesh: row: 32 (over x, y, core), col: 8 (over z).
Axes of the slice: x: 4, y: 4, z: 8, core: 2. Of those that a mesh axis runs over, the one named last changes fastest.
Arguments:
- gradient_rhs: float32 [2, 2048, 240], P(None, 'row'), may hold values from -6 to 6
- pivots: int32 [2048], replicated, may hold values from 0 to 2047, each once
- solved_prev: float32 [2, 131072, 240], P(None, 'row'), may hold values from -6 to 6
- upper_cols: float32 [2, 131072, 2, 1024], P(None, 'row', None, 'col'), may hold values from -0.01171875 to 0.01171875
- upper_coupling: float32 [2, 1024, 1024], P(None, 'row', 'col'), may hold values from -0.125 to 0.125
- block_inverse: float32 [2, 2, 1024, 1024], P(None, None, 'row', 'col'), may hold values from -0.125 to 0.125
Outputs:
- solution: float32 [2, 2, 1024, 240], P(None, None, 'row')
The draws below stay inside these ranges and needn't reach their ends.
Inputs may be any that keep to these rules, and one draw needn't show every extreme that they name: pivots names each of the 2048 rows of gradient_rhs exactly once.
All inputs are finite; a program needn't handle non-finite values.
Results may differ from the reference program's by a relative error of at most 0.00008.
Values sent between devices are 32-bit elements; how exact they have to be, the bound alone decides.
No kernel may reach another device: no remote copies, remote signals or barrier semaphores. Data moves between devices by JAX's collectives and lax.ppermute only.
A program may use at most 64 MiB of HBM per device.

```python
import jax
import jax.numpy as jnp
from jax import lax

NB = 1024
RHS = 240
PREV = 131072


def steps_of(key, extent, shards, low, top_value):
    factor_of = 1.0
    for axis_at, shards_of in shards:
        heights = jax.random.uniform(jax.random.fold_in(jax.random.fold_in(key, 6), axis_at), (shards_of,), jnp.float32, low / len(shards), top_value / len(shards))
        factor_of = factor_of * jnp.repeat(jnp.exp(heights), extent[axis_at] // shards_of).reshape((-1,) + (1,) * (len(extent) - 1 - axis_at))
    return factor_of


def scatter_about(stream_key, shape, spread, most, shards=(), kind=jnp.bfloat16):
    loudness = steps_of(stream_key, shape, shards, -0.22, 0.18) if shards else 1.0
    result = jax.random.normal(stream_key, shape, jnp.float32) * spread * loudness
    return jnp.minimum(jnp.maximum(result, -most), most).astype(kind)


def setup_inputs(seed: int = 0) -> dict:
    seeds = jax.random.split(jax.random.key(seed), 7)
    gradient_rhs = scatter_about(seeds[0], (2, 2 * NB, RHS), 1.0, 6.0, ((1, 32),), jnp.float32)
    pivots = jax.random.permutation(seeds[1], 2 * NB).astype(jnp.int32)
    solved_prev = scatter_about(seeds[2], (2, PREV, RHS), 1.0, 6.0, ((1, 32),), jnp.float32)
    upper_cols = scatter_about(seeds[3], (2, PREV, 2, NB), (2 * PREV) ** -0.5, 0.01171875, ((1, 32), (3, 8)), jnp.float32)
    upper_coupling = scatter_about(seeds[4], (2, NB, NB), (2 * NB) ** -0.5, 0.125, ((1, 32), (2, 8)), jnp.float32)
    block_inverse = scatter_about(seeds[5], (2, 2, NB, NB), (2 * NB) ** -0.5, 0.125, ((2, 32), (3, 8)), jnp.float32)
    return dict(gradient_rhs=gradient_rhs, pivots=pivots, solved_prev=solved_prev, upper_cols=upper_cols, upper_coupling=upper_coupling, block_inverse=block_inverse)


HIGH = lax.Precision.HIGHEST


def contract_cols(matrix, vector):
    return jnp.einsum('pkc,pr->kcr', matrix, vector, precision=HIGH)


def herm_cols(upper_part, solved):
    real_part = contract_cols(upper_part[0], solved[0]) + contract_cols(upper_part[1], solved[1])
    imag_part = contract_cols(upper_part[0], solved[1]) - contract_cols(upper_part[1], solved[0])
    return jnp.stack([real_part, imag_part])


def contract_block(matrix, vector):
    return jnp.einsum('pc,pr->cr', matrix, vector, precision=HIGH)


def herm_block(upper_part, solved):
    real_part = contract_block(upper_part[0], solved[0]) + contract_block(upper_part[1], solved[1])
    imag_part = contract_block(upper_part[0], solved[1]) - contract_block(upper_part[1], solved[0])
    return jnp.stack([real_part, imag_part])


def apply_complex(matrix, vector):
    def mult(left, right):
        return jnp.einsum('nm,mr->nr', left, right, precision=HIGH)
    real_part = mult(matrix[0], vector[0]) - mult(matrix[1], vector[1])
    imag_part = mult(matrix[0], vector[1]) + mult(matrix[1], vector[0])
    return jnp.stack([real_part, imag_part])


def reference(gradient_rhs, pivots, solved_prev, upper_cols, upper_coupling, block_inverse):
    permuted = gradient_rhs[:, pivots, :].reshape(2, 2, NB, RHS)
    column_sums = herm_cols(upper_cols, solved_prev)
    first_block = apply_complex(block_inverse[:, 0], permuted[:, 0] - column_sums[:, 0])
    coupling = herm_block(upper_coupling, first_block)
    second_block = apply_complex(block_inverse[:, 1], permuted[:, 1] - column_sums[:, 1] - coupling)
    return jnp.stack([first_block, second_block], axis=1)
```

```python
import jax
import jax.numpy as jnp
from jax import lax
from jax.experimental import pallas as pl
from jax.experimental.pallas import tpu as pltpu
from jax.sharding import PartitionSpec as P

NB = 1024
RHS = 240
ROWS = 32
CHIPS = 16
COLS = 8
CW = NB // COLS
RW = NB // ROWS
RC = 8
GRAD_ROWS = 2 * NB // ROWS
DEPTH = 512

NN = (((1,), (0,)), ((), ()))
NT = (((1,), (1,)), ((), ()))
TN = (((0,), (0,)), ((), ()))
F32 = jnp.float32
BF16 = jnp.bfloat16


def split(x):
    high = x.astype(BF16)
    return high, (x - high.astype(F32)).astype(BF16)


def dot(left, right, dims):
    return lax.dot_general(left, right, dims, preferred_element_type=F32)


def dot_split(left, right, dims):
    lh, ll = split(left)
    rh, rl = split(right)
    return dot(lh, rh, dims) + (dot(lh, rl, dims) + dot(ll, rh, dims))


def sums_kernel(ids, solved, upper, grad, pivots, out, acc):
    step = pl.program_id(0)

    @pl.when(step == 0)
    def _():
        acc[...] = jnp.zeros_like(acc)

    xh, xl = split(solved[...].reshape(2 * RHS, DEPTH))
    for k in range(2):
        rows = pl.ds(k, DEPTH, stride=2)
        wh, wl = split(jnp.concatenate([upper[0, rows, :], upper[1, rows, :]], axis=1))
        acc[k] += dot(xh, wh, NN) + (dot(xh, wl, NN) + dot(xl, wh, NN))

    @pl.when(step == pl.num_programs(0) - 1)
    def _():
        out[RHS // RC :] = jnp.zeros((ROWS - RHS // RC, 2 * RC, 2 * CW), F32)
        first_row = ids[0] * GRAD_ROWS
        places = lax.broadcasted_iota(jnp.int32, (GRAD_ROWS, CW), 0) + first_row
        for k in range(2):
            target = pivots[pl.ds(k * COLS + ids[1], 1), :]
            chosen = jnp.where(places == target, 1.0, 0.0).astype(BF16)
            re_re, re_im = acc[k, :RHS, :CW], acc[k, :RHS, CW:]
            im_re, im_im = acc[k, RHS:, :CW], acc[k, RHS:, CW:]
            sums = (re_re + im_im, im_re - re_im)
            for c in range(2):
                rest = grad[c].T
                known = jnp.zeros((RHS, CW), F32)
                for _ in range(3):
                    part = rest.astype(BF16)
                    known = known + dot(part, chosen, NN)
                    rest = rest - part.astype(F32)
                term = known - sums[c]
                out[: RHS // RC, c * RC : (c + 1) * RC, k * CW : (k + 1) * CW] = term.reshape(
                    RHS // RC, RC, CW
                )


def column_terms(ids, solved_t, upper_rows, gradient_rhs, pivots):
    depth = solved_t.shape[2]
    return pl.pallas_call(
        sums_kernel,
        out_shape=jax.ShapeDtypeStruct((ROWS, 2 * RC, 2 * CW), F32),
        grid_spec=pltpu.PrefetchScalarGridSpec(
            num_scalar_prefetch=1,
            grid=(depth // DEPTH,),
            in_specs=[
                pl.BlockSpec((2, RHS, DEPTH), lambda s, ids: (0, 0, s)),
                pl.BlockSpec((2, 2 * DEPTH, CW), lambda s, ids: (0, s, 0)),
                pl.BlockSpec((2, GRAD_ROWS, RHS), lambda s, ids: (0, 0, 0)),
                pl.BlockSpec((2 * COLS, CW), lambda s, ids: (0, 0)),
            ],
            out_specs=pl.BlockSpec((ROWS, 2 * RC, 2 * CW), lambda s, ids: (0, 0, 0)),
            scratch_shapes=[pltpu.VMEM((2, 2 * RHS, 2 * CW), F32)],
        ),
        compiler_params=pltpu.CompilerParams(vmem_limit_bytes=40 * 2**20),
        cost_estimate=pl.CostEstimate(
            flops=3 * 8 * RHS * depth * 2 * CW,
            bytes_accessed=4 * (2 * RHS * depth + 4 * depth * CW),
            transcendentals=0,
        ),
        name="column_terms",
    )(ids, solved_t, upper_rows, gradient_rhs, pivots)


def complex_rows(x):
    return jnp.concatenate([x, jnp.concatenate([-x[RC:], x[:RC]], axis=0)], axis=1)


def pair(blocks, which):
    half = CHIPS * RW
    return jnp.concatenate(
        [blocks[:, which].reshape(half, CW), blocks[:, which + 1].reshape(half, CW)], axis=1
    )


def first_kernel(terms, own, other, copies, rhs_second):
    rhs = jnp.sum(terms[...], axis=0)
    rhs_second[...] = rhs[:, CW:]
    left = complex_rows(rhs[:, :CW])
    half = CHIPS * RW
    for at, blocks in enumerate((own, other)):
        share = dot_split(left, pair(blocks, 0), NT)
        for z in range(COLS):
            copies[z, :, at * half : (at + 1) * half] = share


def second_kernel(ids, shares, rhs_second, own, other, packed):
    half = CHIPS * RW
    first = jnp.sum(shares[...], axis=0)
    product = dot_split(first[:, :half], pair(own, 2), NN) + dot_split(
        first[:, half:], pair(other, 2), NN
    )
    coupled = jnp.concatenate(
        [product[:RC, :CW] + product[RC:, CW:], product[RC:, :CW] - product[:RC, CW:]], axis=0
    )
    left = complex_rows(rhs_second[...] - coupled)
    core = lax.rem(ids[0], 2)
    for at, blocks in enumerate((own, other)):
        second = dot_split(left, pair(blocks, 4), NT)
        place = core if at == 0 else 1 - core
        for q in range(CHIPS):
            one = slice(at * half + q * RW, at * half + (q + 1) * RW)
            two = slice(q * RW, (q + 1) * RW)
            packed[2 * q + place] = jnp.concatenate(
                [first[:RC, one], first[RC:, one], second[:RC, two], second[RC:, two]], axis=1
            )


def turn_kernel(packed, first, copies):
    turned = packed[...].reshape(ROWS * RC, 4 * RW).T
    first[...] = turned[: 2 * RW]
    for z in range(COLS):
        copies[z] = turned[2 * RW :]


def join_kernel(first, shares, out):
    second = jnp.sum(shares[...], axis=0)
    for c in range(2):
        out[c, 0] = first[c * RW : (c + 1) * RW, :RHS]
        out[c, 1] = second[c * RW : (c + 1) * RW, :RHS]


VMEM = pl.BlockSpec(memory_space=pltpu.VMEM)
SMEM = pl.BlockSpec(memory_space=pltpu.SMEM)


def local(kernel, ins, shapes, name):
    return pl.pallas_call(
        kernel,
        in_specs=ins,
        out_specs=[VMEM] * len(shapes),
        out_shape=[jax.ShapeDtypeStruct(s, F32) for s in shapes],
        compiler_params=pltpu.CompilerParams(vmem_limit_bytes=24 * 2**20),
        name=name,
    )


SAME_CORE = [[2 * q + c for q in range(CHIPS)] for c in range(2)]
OTHER_CORE = [(i, i ^ 1) for i in range(ROWS)]


def exchange(x, axis, groups=None):
    return lax.all_to_all(x, axis, 0, 0, axis_index_groups=groups, tiled=True)


def on_device(gradient_rhs, pivots, solved_prev, upper_cols, upper_coupling, block_inverse):
    row = lax.axis_index("row")
    ids = jnp.stack([row, lax.axis_index("col")]).astype(jnp.int32)

    mine = jnp.concatenate([block_inverse[:, 0], upper_coupling, block_inverse[:, 1]], axis=0)
    own = exchange(jnp.broadcast_to(mine[None], (CHIPS,) + mine.shape), "row", SAME_CORE)
    other = lax.ppermute(own, "row", OTHER_CORE)

    terms = column_terms(
        ids,
        jnp.swapaxes(solved_prev, 1, 2),
        upper_cols.reshape(2, -1, CW),
        gradient_rhs,
        pivots.reshape(2 * COLS, CW),
    )
    terms = exchange(terms, "row")
    copies, rhs_second = local(
        first_kernel, [VMEM] * 3, [(COLS, 2 * RC, NB), (2 * RC, CW)], "first_share"
    )(terms, own, other)
    shares = exchange(copies, "col")
    (packed,) = local(
        second_kernel, [SMEM] + [VMEM] * 4, [(ROWS, RC, 4 * RW)], "second_share"
    )(ids, shares, rhs_second, own, other)
    packed = exchange(packed, "row")
    first, copies = local(
        turn_kernel, [VMEM], [(2 * RW, ROWS * RC), (COLS, 2 * RW, ROWS * RC)], "turn"
    )(packed)
    shares = exchange(copies, "col")
    (solved,) = local(join_kernel, [VMEM] * 2, [(2, 2, RW, RHS)], "join")(first, shares)
    return solved


def solution(mesh):
    placed = (
        P(None, "row", None),
        P(),
        P(None, "row", None),
        P(None, "row", None, "col"),
        P(None, "row", "col"),
        P(None, None, "row", "col"),
    )
    return jax.shard_map(
        on_device, mesh=mesh, in_specs=placed, out_specs=P(None, None, "row", None), check_vma=False
    )
```

```python
import jax
import jax.numpy as jnp
from jax import lax
from jax.experimental import pallas as pl
from jax.experimental.pallas import tpu as pltpu
from jax.sharding import PartitionSpec as P

NB = 1024
RHS = 240
ROWS = 32
CHIPS = 16
COLS = 8
CW = NB // COLS
RW = NB // ROWS
RC = 8
GRAD_ROWS = 2 * NB // ROWS
DEPTH = 512
AHEAD = 3

NN = (((1,), (0,)), ((), ()))
NT = (((1,), (1,)), ((), ()))
TN = (((0,), (0,)), ((), ()))
F32 = jnp.float32
BF16 = jnp.bfloat16
VMEM = pl.BlockSpec(memory_space=pltpu.VMEM)
ANY = pl.BlockSpec(memory_space=pl.ANY)


def split(x):
    high = x.astype(BF16)
    return high, (x - high.astype(F32)).astype(BF16)


def dot(left, right, dims):
    return lax.dot_general(left, right, dims, preferred_element_type=F32)


def dot_split(left, right, dims):
    lh, ll = split(left)
    rh, rl = split(right)
    return dot(lh, rh, dims) + (dot(lh, rl, dims) + dot(ll, rh, dims))


def prepare_kernel(inverse, coupling, copies, arrived):
    loads = (
        pltpu.make_async_copy(inverse.at[:, 0], copies.at[0, pl.ds(0, 2)], arrived.at[0]),
        pltpu.make_async_copy(coupling, copies.at[0, pl.ds(2, 2)], arrived.at[1]),
    )
    for load in loads:
        load.start()
    for load in loads:
        load.wait()
    copies[1:] = jnp.broadcast_to(copies[0], (CHIPS - 1, 4, RW, CW))


def known_terms(grad, pivots, out):
    first_row = lax.axis_index("row") * GRAD_ROWS
    places = lax.broadcasted_iota(jnp.int32, (GRAD_ROWS, CW), 0) + first_row
    for k in range(2):
        target = pivots[pl.ds(k * COLS + lax.axis_index("col"), 1), :]
        chosen = jnp.where(places == target, 1.0, 0.0).astype(BF16)
        for c in range(2):
            rest = grad[c].T
            known = jnp.zeros((RHS, CW), F32)
            for _ in range(3):
                part = rest.astype(BF16)
                known = known + dot(part, chosen, NN)
                rest = rest - part.astype(F32)
            out[: RHS // RC, c * RC : (c + 1) * RC, k * CW : (k + 1) * CW] = known.reshape(
                RHS // RC, RC, CW
            )


def sums_kernel(solved, upper, grad, pivots, mine, theirs, vectors, blocks, acc, out, arrived):
    steps = solved.shape[2] // DEPTH

    def loads(s):
        cols, rows = pl.ds(s * DEPTH, DEPTH), pl.ds(s * 2 * DEPTH, 2 * DEPTH)
        return (
            pltpu.make_async_copy(
                solved.at[:, :, cols], vectors.at[:, :, cols], arrived.at[0, s]
            ),
            pltpu.make_async_copy(upper.at[:, rows, :], blocks.at[:, rows, :], arrived.at[1, s]),
        )

    for s in range(AHEAD):
        for load in loads(s):
            load.start()
    acc[...] = jnp.zeros_like(acc)
    out[RHS // RC :] = jnp.zeros((ROWS - RHS // RC, 2 * RC, 2 * CW), F32)
    known_terms(grad, pivots, out)
    for s in range(steps):
        for load in loads(s):
            load.wait()
        if s + AHEAD < steps:
            for load in loads(s + AHEAD):
                load.start()
        xh, xl = split(vectors[:, :, s * DEPTH : (s + 1) * DEPTH].reshape(2 * RHS, DEPTH))
        for k in range(2):
            rows = pl.ds(s * 2 * DEPTH + k, DEPTH, stride=2)
            wh, wl = split(jnp.concatenate([blocks[0, rows, :], blocks[1, rows, :]], axis=1))
            acc[k] += dot(xh, wh, NN) + (dot(xh, wl, NN) + dot(xl, wh, NN))

    for k in range(2):
        re_re, re_im = acc[k, :RHS, :CW], acc[k, :RHS, CW:]
        im_re, im_im = acc[k, RHS:, :CW], acc[k, RHS:, CW:]
        for c, sums in enumerate((re_re + im_im, im_re - re_im)):
            place = (
                slice(0, RHS // RC),
                slice(c * RC, (c + 1) * RC),
                slice(k * CW, (k + 1) * CW),
            )
            out[place] = out[place] - sums.reshape(RHS // RC, RC, CW)
    core = lax.rem(lax.axis_index("row"), 2)
    mine[...] = out[pl.ds(core * CHIPS, CHIPS)]
    theirs[...] = out[pl.ds((1 - core) * CHIPS, CHIPS)]


def column_terms(solved_t, upper_rows, gradient_rhs, pivots):
    depth = solved_t.shape[2]
    return pl.pallas_call(
        sums_kernel,
        out_shape=[jax.ShapeDtypeStruct((CHIPS, 2 * RC, 2 * CW), F32)] * 2,
        in_specs=[ANY, ANY, VMEM, VMEM],
        out_specs=[VMEM] * 2,
        scratch_shapes=[
            pltpu.VMEM((2, RHS, depth), F32),
            pltpu.VMEM((2, 2 * depth, CW), F32),
            pltpu.VMEM((2, 2 * RHS, 2 * CW), F32),
            pltpu.VMEM((ROWS, 2 * RC, 2 * CW), F32),
            pltpu.SemaphoreType.DMA((2, depth // DEPTH)),
        ],
        compiler_params=pltpu.CompilerParams(vmem_limit_bytes=56 * 2**20),
        cost_estimate=pl.CostEstimate(
            flops=3 * 8 * RHS * depth * 2 * CW,
            bytes_accessed=4 * (2 * RHS * depth + 4 * depth * CW),
            transcendentals=0,
        ),
        name="column_terms",
    )(solved_t, upper_rows, gradient_rhs, pivots)


def complex_rows(x):
    return jnp.concatenate([x, jnp.concatenate([-x[RC:], x[:RC]], axis=0)], axis=1)


def pair(blocks, which):
    half = CHIPS * RW
    return jnp.concatenate(
        [blocks[:, which].reshape(half, CW), blocks[:, which + 1].reshape(half, CW)], axis=1
    )


def first_kernel(terms, own, other, copies, rhs_second):
    rhs = jnp.sum(terms[...], axis=0)
    rhs_second[...] = rhs[:, CW:]
    left = complex_rows(rhs[:, :CW])
    half = CHIPS * RW
    for at, blocks in enumerate((own, other)):
        share = dot_split(left, pair(blocks, 0), NT)
        for z in range(COLS):
            copies[z, :, at * half : (at + 1) * half] = share


def coupling_kernel(shares, rhs_second, own, other, packed):
    half = CHIPS * RW
    first = jnp.sum(shares[...], axis=0)
    product = dot_split(first[:, :half], pair(own, 2), NN) + dot_split(
        first[:, half:], pair(other, 2), NN
    )
    coupled = jnp.concatenate(
        [product[:RC, :CW] + product[RC:, CW:], product[RC:, :CW] - product[:RC, CW:]], axis=0
    )
    packed[:, : 2 * RC] = jnp.broadcast_to(rhs_second[...] - coupled, (ROWS, 2 * RC, CW))
    core = lax.rem(lax.axis_index("row"), 2)
    for at in range(2):
        place = core if at == 0 else 1 - core
        for q in range(CHIPS):
            one = slice(at * half + q * RW, at * half + (q + 1) * RW)
            packed[2 * q + place, 2 * RC :] = jnp.concatenate(
                [first[:RC, one], first[RC:, one], jnp.zeros((RC, CW - 2 * RW), F32)], axis=1
            )


def second_kernel(packed, inverse, first, copies):
    def ordered(part):
        chunks = packed[:, part * RC : (part + 1) * RC].reshape(CHIPS, 2, RC, CW)
        return jnp.concatenate([chunks[:, h].reshape(CHIPS * RC, CW) for h in range(2)], axis=0)

    rhs = jnp.concatenate([ordered(0), ordered(1)], axis=1)
    real, imaginary = inverse[0, 1], inverse[1, 1]
    left = jnp.concatenate(
        [
            jnp.concatenate([real, -imaginary], axis=1),
            jnp.concatenate([imaginary, real], axis=1),
        ],
        axis=0,
    )
    share = dot_split(left, rhs, NT)
    for z in range(COLS):
        copies[z] = share
    first[...] = ordered(2).T[: 2 * RW]


def join_kernel(first, shares, out):
    second = jnp.sum(shares[...], axis=0)
    for c in range(2):
        out[c, 0] = first[c * RW : (c + 1) * RW, :RHS]
        out[c, 1] = second[c * RW : (c + 1) * RW, :RHS]


def local(kernel, ins, shapes, name, scratch=(), limit=24):
    return pl.pallas_call(
        kernel,
        in_specs=ins,
        out_specs=[VMEM] * len(shapes),
        out_shape=[jax.ShapeDtypeStruct(s, F32) for s in shapes],
        scratch_shapes=scratch,
        compiler_params=pltpu.CompilerParams(vmem_limit_bytes=limit * 2**20),
        name=name,
    )


SAME_CORE = [[2 * q + c for q in range(CHIPS)] for c in range(2)]
OTHER_CORE = [(i, i ^ 1) for i in range(ROWS)]


def exchange(x, axis, groups=None):
    return lax.all_to_all(x, axis, 0, 0, axis_index_groups=groups, tiled=True)


def on_device(gradient_rhs, pivots, solved_prev, upper_cols, upper_coupling, block_inverse):
    (copies,) = local(
        prepare_kernel,
        [ANY] * 2,
        [(CHIPS, 4, RW, CW)],
        "prepare",
        [pltpu.SemaphoreType.DMA((2,))],
        limit=56,
    )(block_inverse, upper_coupling)
    own = exchange(copies, "row", SAME_CORE)

    mine, theirs = column_terms(
        jnp.swapaxes(solved_prev, 1, 2),
        upper_cols.reshape(2, -1, CW),
        gradient_rhs,
        pivots.reshape(2 * COLS, CW),
    )
    terms = mine + lax.ppermute(theirs, "row", OTHER_CORE)
    own, terms = lax.optimization_barrier((own, terms))
    other = lax.ppermute(own, "row", OTHER_CORE)
    terms = exchange(terms, "row", SAME_CORE)
    copies, rhs_second = local(
        first_kernel, [VMEM] * 3, [(COLS, 2 * RC, NB), (2 * RC, CW)], "first_share"
    )(terms, own, other)
    shares = exchange(copies, "col")
    (packed,) = local(
        coupling_kernel, [VMEM] * 4, [(ROWS, 3 * RC, CW)], "coupling"
    )(shares, rhs_second, own, other)
    packed = exchange(packed, "row")
    first, copies = local(
        second_kernel, [VMEM] * 2, [(2 * RW, ROWS * RC), (COLS, 2 * RW, ROWS * RC)], "second_share"
    )(packed, block_inverse)
    shares = exchange(copies, "col")
    (solved,) = local(join_kernel, [VMEM] * 2, [(2, 2, RW, RHS)], "join")(first, shares)
    return solved


def solution(mesh):
    placed = (
        P(None, "row", None),
        P(),
        P(None, "row", None),
        P(None, "row", None, "col"),
        P(None, "row", "col"),
        P(None, None, "row", "col"),
    )
    return jax.shard_map(
        on_device, mesh=mesh, in_specs=placed, out_specs=P(None, None, "row", None), check_vma=False
    )
```

```python
import jax
import jax.numpy as jnp
from jax import lax
from jax.experimental import pallas as pl
from jax.experimental.pallas import tpu as pltpu
from jax.sharding import PartitionSpec as P

NB = 1024
RHS = 240
ROWS = 32
CHIPS = 16
COLS = 8
CW = NB // COLS
RW = NB // ROWS
RC = 8
GRAD_ROWS = 2 * NB // ROWS
DEPTH = 512
AHEAD = 3

NN = (((1,), (0,)), ((), ()))
NT = (((1,), (1,)), ((), ()))
TN = (((0,), (0,)), ((), ()))
F32 = jnp.float32
BF16 = jnp.bfloat16
VMEM = pl.BlockSpec(memory_space=pltpu.VMEM)
HBM = pl.BlockSpec(memory_space=pl.ANY)


def split(x):
    high = x.astype(BF16)
    return high, (x - high.astype(F32)).astype(BF16)


def dot(left, right, dims):
    return lax.dot_general(left, right, dims, preferred_element_type=F32)


def dot_split(left, right, dims):
    lh, ll = split(left)
    rh, rl = split(right)
    return dot(lh, rh, dims) + (dot(lh, rl, dims) + dot(ll, rh, dims))


def prepare_kernel(inverse, coupling, copies, mine, arrived, sent):
    loads = (
        pltpu.make_async_copy(inverse.at[:, 0], mine.at[pl.ds(0, 2)], arrived.at[0]),
        pltpu.make_async_copy(coupling, mine.at[pl.ds(2, 2)], arrived.at[1]),
    )
    for load in loads:
        load.start()
    for load in loads:
        load.wait()
    stores = [pltpu.make_async_copy(mine, copies.at[q], sent.at[q]) for q in range(CHIPS)]
    for store in stores:
        store.start()
    for store in stores:
        store.wait()


def known_terms(grad, pivots, known):
    first_row = lax.axis_index("row") * GRAD_ROWS
    places = lax.broadcasted_iota(jnp.int32, (GRAD_ROWS, CW), 0) + first_row
    for k in range(2):
        target = pivots[pl.ds(k * COLS + lax.axis_index("col"), 1), :]
        chosen = jnp.where(places == target, 1.0, 0.0).astype(BF16)
        for c in range(2):
            rest = grad[c].T
            rows = jnp.zeros((RHS, CW), F32)
            for _ in range(3):
                part = rest.astype(BF16)
                rows = rows + dot(part, chosen, NN)
                rest = rest - part.astype(F32)
            known[:, c * RC : (c + 1) * RC, k * CW : (k + 1) * CW] = rows.reshape(
                RHS // RC, RC, CW
            )


def sums_kernel(
    solved, upper, gradient_rhs, all_pivots, mine, theirs, vectors, blocks, grad, pivots, acc, known, arrived
):
    steps = solved.shape[2] // DEPTH

    def loads(s):
        cols, rows = pl.ds(s * DEPTH, DEPTH), pl.ds(s * 2 * DEPTH, 2 * DEPTH)
        return (
            pltpu.make_async_copy(
                solved.at[:, :, cols], vectors.at[:, :, cols], arrived.at[0, s]
            ),
            pltpu.make_async_copy(upper.at[:, rows, :], blocks.at[:, rows, :], arrived.at[1, s]),
        )

    small = (
        pltpu.make_async_copy(gradient_rhs, grad, arrived.at[0, steps]),
        pltpu.make_async_copy(all_pivots, pivots, arrived.at[1, steps]),
    )
    for load in small:
        load.start()
    for s in range(AHEAD):
        for load in loads(s):
            load.start()
    for load in small:
        load.wait()
    known_terms(grad, pivots, known)
    for s in range(steps):
        for load in loads(s):
            load.wait()
        if s + AHEAD < steps:
            for load in loads(s + AHEAD):
                load.start()
        xh, xl = split(vectors[:, :, s * DEPTH : (s + 1) * DEPTH].reshape(2 * RHS, DEPTH))
        for k in range(2):
            rows = pl.ds(s * 2 * DEPTH + k, DEPTH, stride=2)
            wh, wl = split(jnp.concatenate([blocks[0, rows, :], blocks[1, rows, :]], axis=1))
            product = dot(xh, wh, NN) + (dot(xh, wl, NN) + dot(xl, wh, NN))
            acc[k] = product if s == 0 else acc[k] + product

    def close(half, to):
        first, last = half * CHIPS * RC, min((half + 1) * CHIPS * RC, RHS)
        chunks = (last - first) // RC
        for k in range(2):
            panel = slice(k * CW, (k + 1) * CW)
            re_re, re_im = (acc[k, first:last, at * CW : (at + 1) * CW] for at in range(2))
            im_re, im_im = (
                acc[k, RHS + first : RHS + last, at * CW : (at + 1) * CW] for at in range(2)
            )
            for c, sums in enumerate((re_re + im_im, im_re - re_im)):
                rows = slice(c * RC, (c + 1) * RC)
                to[:chunks, rows, panel] = known[
                    first // RC : last // RC, rows, panel
                ] - sums.reshape(chunks, RC, CW)
        if chunks < CHIPS:
            to[chunks:] = jnp.zeros((CHIPS - chunks, 2 * RC, 2 * CW), F32)

    core = lax.rem(lax.axis_index("row"), 2)
    for half in range(2):

        @pl.when(core == half)
        def _():
            close(half, mine)
            close(1 - half, theirs)


def column_terms(solved_t, upper_rows, gradient_rhs, pivots):
    depth = solved_t.shape[2]
    return pl.pallas_call(
        sums_kernel,
        out_shape=[jax.ShapeDtypeStruct((CHIPS, 2 * RC, 2 * CW), F32)] * 2,
        in_specs=[HBM] * 4,
        out_specs=[VMEM] * 2,
        scratch_shapes=[
            pltpu.VMEM((2, RHS, depth), F32),
            pltpu.VMEM((2, 2 * depth, CW), F32),
            pltpu.VMEM((2, GRAD_ROWS, RHS), F32),
            pltpu.VMEM((2 * COLS, CW), jnp.int32),
            pltpu.VMEM((2, 2 * RHS, 2 * CW), F32),
            pltpu.VMEM((RHS // RC, 2 * RC, 2 * CW), F32),
            pltpu.SemaphoreType.DMA((2, depth // DEPTH + 1)),
        ],
        compiler_params=pltpu.CompilerParams(vmem_limit_bytes=50 * 2**20),
        cost_estimate=pl.CostEstimate(
            flops=3 * 8 * RHS * depth * 2 * CW,
            bytes_accessed=4 * (2 * RHS * depth + 4 * depth * CW),
            transcendentals=0,
        ),
        name="column_terms",
    )(solved_t, upper_rows, gradient_rhs, pivots)


def complex_rows(x):
    return jnp.concatenate([x, jnp.concatenate([-x[RC:], x[:RC]], axis=0)], axis=1)


def pair(blocks, which):
    half = CHIPS * RW
    return jnp.concatenate(
        [blocks[:, which].reshape(half, CW), blocks[:, which + 1].reshape(half, CW)], axis=1
    )


def first_kernel(terms, own, other, copies, rhs_second):
    rhs = jnp.sum(terms[...], axis=0)
    rhs_second[...] = rhs[:, CW:]
    left = complex_rows(rhs[:, :CW])
    half = CHIPS * RW
    for at, blocks in enumerate((own, other)):
        share = dot_split(left, pair(blocks, 0), NT)
        for z in range(COLS):
            copies[z, :, at * half : (at + 1) * half] = share


def coupling_kernel(shares, rhs_second, own, other, packed):
    half = CHIPS * RW
    first = jnp.sum(shares[...], axis=0)
    product = dot_split(first[:, :half], pair(own, 2), NN) + dot_split(
        first[:, half:], pair(other, 2), NN
    )
    coupled = jnp.concatenate(
        [product[:RC, :CW] + product[RC:, CW:], product[RC:, :CW] - product[:RC, CW:]], axis=0
    )
    packed[:, : 2 * RC] = jnp.broadcast_to(rhs_second[...] - coupled, (CHIPS, 2 * RC, CW))
    for q in range(CHIPS):
        one = slice(q * RW, (q + 1) * RW)
        two = slice(half + q * RW, half + (q + 1) * RW)
        packed[q, 2 * RC :] = jnp.concatenate(
            [first[:RC, one], first[RC:, one], first[:RC, two], first[RC:, two]], axis=1
        )


def second_kernel(mine, theirs, inverse, first, copies):
    real, imaginary = inverse[0, 1], inverse[1, 1]
    left = jnp.concatenate(
        [
            jnp.concatenate([real, -imaginary], axis=1),
            jnp.concatenate([imaginary, real], axis=1),
        ],
        axis=0,
    )
    shares, rows = [], []
    for at, got in enumerate((mine, theirs)):
        parts = [got[:, p * RC : (p + 1) * RC].reshape(CHIPS * RC, CW) for p in range(3)]
        shares.append(dot_split(left, jnp.concatenate(parts[:2], axis=1), NT))
        rows.append(parts[2].T[at * 2 * RW : (at + 1) * 2 * RW])
    core = lax.rem(lax.axis_index("row"), 2)
    for half in range(2):
        place = slice(half * CHIPS * RC, (half + 1) * CHIPS * RC)
        first[:, place] = jnp.where(core == half, rows[0], rows[1])
        share = jnp.where(core == half, shares[0], shares[1])
        for z in range(COLS):
            copies[z, :, place] = share


def join_kernel(first, shares, out):
    second = jnp.sum(shares[...], axis=0)
    for c in range(2):
        out[c, 0] = first[c * RW : (c + 1) * RW, :RHS]
        out[c, 1] = second[c * RW : (c + 1) * RW, :RHS]


def local(kernel, ins, shapes, name, scratch=(), limit=24):
    return pl.pallas_call(
        kernel,
        in_specs=ins,
        out_specs=[VMEM] * len(shapes),
        out_shape=[jax.ShapeDtypeStruct(s, F32) for s in shapes],
        scratch_shapes=scratch,
        compiler_params=pltpu.CompilerParams(vmem_limit_bytes=limit * 2**20),
        name=name,
    )


SAME_CORE = [[2 * q + c for q in range(CHIPS)] for c in range(2)]
OTHER_CORE = [(i, i ^ 1) for i in range(ROWS)]


def exchange(x, axis, groups=None):
    return lax.all_to_all(x, axis, 0, 0, axis_index_groups=groups, tiled=True)


def on_device(gradient_rhs, pivots, solved_prev, upper_cols, upper_coupling, block_inverse):
    copies = pl.pallas_call(
        prepare_kernel,
        in_specs=[HBM] * 2,
        out_specs=HBM,
        out_shape=jax.ShapeDtypeStruct((CHIPS, 4, RW, CW), F32),
        scratch_shapes=[
            pltpu.VMEM((4, RW, CW), F32),
            pltpu.SemaphoreType.DMA((2,)),
            pltpu.SemaphoreType.DMA((CHIPS,)),
        ],
        compiler_params=pltpu.CompilerParams(vmem_limit_bytes=56 * 2**20),
        cost_estimate=pl.CostEstimate(flops=10**10, bytes_accessed=2**25, transcendentals=0),
        name="prepare",
    )(block_inverse, upper_coupling)
    own = exchange(copies, "row", SAME_CORE)

    mine, theirs = column_terms(
        jnp.swapaxes(solved_prev, 1, 2),
        upper_cols.reshape(2, -1, CW),
        gradient_rhs,
        pivots.reshape(2 * COLS, CW),
    )
    terms = mine + lax.ppermute(theirs, "row", OTHER_CORE)
    own, terms = lax.optimization_barrier((own, terms))
    other = lax.ppermute(own, "row", OTHER_CORE)
    terms = exchange(terms, "row", SAME_CORE)
    copies, rhs_second = local(
        first_kernel, [VMEM] * 3, [(COLS, 2 * RC, NB), (2 * RC, CW)], "first_share"
    )(terms, own, other)
    shares = exchange(copies, "col")
    (packed,) = local(
        coupling_kernel, [VMEM] * 4, [(CHIPS, 3 * RC, CW)], "coupling"
    )(shares, rhs_second, own, other)
    mine = exchange(packed, "row", SAME_CORE)
    theirs = lax.ppermute(mine, "row", OTHER_CORE)
    first, copies = local(
        second_kernel, [VMEM] * 3, [(2 * RW, ROWS * RC), (COLS, 2 * RW, ROWS * RC)], "second_share"
    )(mine, theirs, block_inverse)
    shares = exchange(copies, "col")
    (solved,) = local(join_kernel, [VMEM] * 2, [(2, 2, RW, RHS)], "join")(first, shares)
    return solved


def solution(mesh):
    placed = (
        P(None, "row", None),
        P(),
        P(None, "row", None),
        P(None, "row", None, "col"),
        P(None, "row", "col"),
        P(None, None, "row", "col"),
    )
    return jax.shard_map(
        on_device, mesh=mesh, in_specs=placed, out_specs=P(None, None, "row", None), check_vma=False
    )
```

```python
import jax
import jax.numpy as jnp
from jax import lax
from jax.experimental import pallas as pl
from jax.experimental.pallas import tpu as pltpu
from jax.sharding import PartitionSpec as P

NB = 1024
RHS = 240
ROWS = 32
CHIPS = 16
COLS = 8
CW = NB // COLS
RW = NB // ROWS
RC = 8
LANES = 128
TAIL = RHS - LANES
FREE = LANES - TAIL
GROUPS = 2 * RW // 8
GRAD_ROWS = 2 * NB // ROWS
DEPTH = 512
AHEAD = 3

NN = (((1,), (0,)), ((), ()))
NT = (((1,), (1,)), ((), ()))
TN = (((0,), (0,)), ((), ()))
F32 = jnp.float32
BF16 = jnp.bfloat16
VMEM = pl.BlockSpec(memory_space=pltpu.VMEM)
HBM = pl.BlockSpec(memory_space=pl.ANY)


def split(x):
    high = x.astype(BF16)
    return high, (x - high.astype(F32)).astype(BF16)


def dot(left, right, dims):
    return lax.dot_general(left, right, dims, preferred_element_type=F32)


def dot_split(left, right, dims):
    lh, ll = split(left)
    rh, rl = split(right)
    return dot(lh, rh, dims) + (dot(lh, rl, dims) + dot(ll, rh, dims))


def prepare_kernel(inverse, coupling, copies, mine, arrived, sent):
    loads = (
        pltpu.make_async_copy(inverse.at[:, 0], mine.at[pl.ds(0, 2)], arrived.at[0]),
        pltpu.make_async_copy(coupling, mine.at[pl.ds(2, 2)], arrived.at[1]),
    )
    for load in loads:
        load.start()
    for load in loads:
        load.wait()
    stores = [pltpu.make_async_copy(mine, copies.at[q], sent.at[q]) for q in range(CHIPS)]
    for store in stores:
        store.start()
    for store in stores:
        store.wait()


def known_terms(grad, pivots, known):
    first_row = lax.axis_index("row") * GRAD_ROWS
    places = lax.broadcasted_iota(jnp.int32, (GRAD_ROWS, CW), 0) + first_row
    for k in range(2):
        target = pivots[pl.ds(k * COLS + lax.axis_index("col"), 1), :]
        chosen = jnp.where(places == target, 1.0, 0.0).astype(BF16)
        for c in range(2):
            rest = grad[c].T
            rows = jnp.zeros((RHS, CW), F32)
            for _ in range(3):
                part = rest.astype(BF16)
                rows = rows + dot(part, chosen, NN)
                rest = rest - part.astype(F32)
            known[:, c * RC : (c + 1) * RC, k * CW : (k + 1) * CW] = rows.reshape(
                RHS // RC, RC, CW
            )


def sums_kernel(
    solved, upper, gradient_rhs, all_pivots, mine, theirs, vectors, blocks, grad, pivots, acc, known, arrived
):
    steps = solved.shape[2] // DEPTH

    def loads(s):
        cols, rows = pl.ds(s * DEPTH, DEPTH), pl.ds(s * 2 * DEPTH, 2 * DEPTH)
        return (
            pltpu.make_async_copy(
                solved.at[:, :, cols], vectors.at[:, :, cols], arrived.at[0, s]
            ),
            pltpu.make_async_copy(upper.at[:, rows, :], blocks.at[:, rows, :], arrived.at[1, s]),
        )

    small = (
        pltpu.make_async_copy(gradient_rhs, grad, arrived.at[0, steps]),
        pltpu.make_async_copy(all_pivots, pivots, arrived.at[1, steps]),
    )
    for load in small:
        load.start()
    for s in range(AHEAD):
        for load in loads(s):
            load.start()
    for load in small:
        load.wait()
    known_terms(grad, pivots, known)
    for s in range(steps):
        for load in loads(s):
            load.wait()
        if s + AHEAD < steps:
            for load in loads(s + AHEAD):
                load.start()
        xh, xl = split(vectors[:, :, s * DEPTH : (s + 1) * DEPTH].reshape(2 * RHS, DEPTH))
        for k in range(2):
            rows = pl.ds(s * 2 * DEPTH + k, DEPTH, stride=2)
            wh, wl = split(jnp.concatenate([blocks[0, rows, :], blocks[1, rows, :]], axis=1))
            product = dot(xh, wh, NN) + (dot(xh, wl, NN) + dot(xl, wh, NN))
            acc[k] = product if s == 0 else acc[k] + product

    def close(half, to):
        first, last = half * CHIPS * RC, min((half + 1) * CHIPS * RC, RHS)
        chunks = (last - first) // RC
        for k in range(2):
            panel = slice(k * CW, (k + 1) * CW)
            re_re, re_im = (acc[k, first:last, at * CW : (at + 1) * CW] for at in range(2))
            im_re, im_im = (
                acc[k, RHS + first : RHS + last, at * CW : (at + 1) * CW] for at in range(2)
            )
            for c, sums in enumerate((re_re + im_im, im_re - re_im)):
                rows = slice(c * RC, (c + 1) * RC)
                to[:chunks, rows, panel] = known[
                    first // RC : last // RC, rows, panel
                ] - sums.reshape(chunks, RC, CW)
        if chunks < CHIPS:
            to[chunks:] = jnp.zeros((CHIPS - chunks, 2 * RC, 2 * CW), F32)

    core = lax.rem(lax.axis_index("row"), 2)
    for half in range(2):

        @pl.when(core == half)
        def _():
            close(half, mine)
            close(1 - half, theirs)


def column_terms(solved_t, upper_rows, gradient_rhs, pivots):
    depth = solved_t.shape[2]
    return pl.pallas_call(
        sums_kernel,
        out_shape=[jax.ShapeDtypeStruct((CHIPS, 2 * RC, 2 * CW), F32)] * 2,
        in_specs=[HBM] * 4,
        out_specs=[VMEM] * 2,
        scratch_shapes=[
            pltpu.VMEM((2, RHS, depth), F32),
            pltpu.VMEM((2, 2 * depth, CW), F32),
            pltpu.VMEM((2, GRAD_ROWS, RHS), F32),
            pltpu.VMEM((2 * COLS, CW), jnp.int32),
            pltpu.VMEM((2, 2 * RHS, 2 * CW), F32),
            pltpu.VMEM((RHS // RC, 2 * RC, 2 * CW), F32),
            pltpu.SemaphoreType.DMA((2, depth // DEPTH + 1)),
        ],
        compiler_params=pltpu.CompilerParams(vmem_limit_bytes=50 * 2**20),
        cost_estimate=pl.CostEstimate(
            flops=3 * 8 * RHS * depth * 2 * CW,
            bytes_accessed=4 * (2 * RHS * depth + 4 * depth * CW),
            transcendentals=0,
        ),
        name="column_terms",
    )(solved_t, upper_rows, gradient_rhs, pivots)


def complex_rows(x):
    return jnp.concatenate([x, jnp.concatenate([-x[RC:], x[:RC]], axis=0)], axis=1)


def pair(blocks, which):
    half = CHIPS * RW
    return jnp.concatenate(
        [blocks[:, which].reshape(half, CW), blocks[:, which + 1].reshape(half, CW)], axis=1
    )


def first_kernel(terms, own, other, copies, rhs_second):
    rhs = jnp.sum(terms[...], axis=0)
    rhs_second[...] = rhs[:, CW:]
    left = complex_rows(rhs[:, :CW])
    half = CHIPS * RW
    for at, blocks in enumerate((own, other)):
        share = dot_split(left, pair(blocks, 0), NT)
        for z in range(COLS):
            copies[z, :, at * half : (at + 1) * half] = share


def coupling_kernel(shares, rhs_second, own, other, packed):
    half = CHIPS * RW
    first = jnp.sum(shares[...], axis=0)
    product = dot_split(first[:, :half], pair(own, 2), NN) + dot_split(
        first[:, half:], pair(other, 2), NN
    )
    coupled = jnp.concatenate(
        [product[:RC, :CW] + product[RC:, CW:], product[RC:, :CW] - product[:RC, CW:]], axis=0
    )
    packed[:, : 2 * RC] = jnp.broadcast_to(rhs_second[...] - coupled, (CHIPS, 2 * RC, CW))
    for q in range(CHIPS):
        one = slice(q * RW, (q + 1) * RW)
        two = slice(half + q * RW, half + (q + 1) * RW)
        packed[q, 2 * RC :] = jnp.concatenate(
            [first[:RC, one], first[RC:, one], first[:RC, two], first[RC:, two]], axis=1
        )


def second_kernel(mine, theirs, inverse, first, copies):
    real, imaginary = inverse[0, 1], inverse[1, 1]
    left = jnp.concatenate(
        [
            jnp.concatenate([real, -imaginary], axis=1),
            jnp.concatenate([imaginary, real], axis=1),
        ],
        axis=0,
    )
    shares, rows = [], []
    for at, got in enumerate((mine, theirs)):
        parts = [got[:, p * RC : (p + 1) * RC].reshape(CHIPS * RC, CW) for p in range(3)]
        shares.append(dot_split(left, jnp.concatenate(parts[:2], axis=1), NT))
        rows.append(parts[2].T[at * 2 * RW : (at + 1) * 2 * RW])
    core = lax.rem(lax.axis_index("row"), 2)
    for half in range(2):
        place = slice(half * CHIPS * RC, (half + 1) * CHIPS * RC)
        first[:, place] = jnp.where(core == half, rows[0], rows[1])
        share = jnp.where(core == half, shares[0], shares[1])
        if half == 0:
            tiles = [share]
        else:
            tiles += [
                jnp.concatenate(
                    [share[g * 8 : (g + 1) * 8, :TAIL], share[-8:, g * FREE : (g + 1) * FREE]],
                    axis=1,
                )
                for g in range(GROUPS - 1)
            ]
    packed = jnp.concatenate(tiles, axis=0)
    for z in range(COLS):
        copies[z] = packed


def join_kernel(first, shares, out):
    second = jnp.sum(shares[...], axis=0)
    tails = [second[2 * RW + g * 8 : 2 * RW + (g + 1) * 8] for g in range(GROUPS - 1)]
    last = jnp.concatenate([tail[:, TAIL:] for tail in tails], axis=1)
    tail = jnp.concatenate([tail[:, :TAIL] for tail in tails] + [last], axis=0)
    for c in range(2):
        rows = slice(c * RW, (c + 1) * RW)
        out[c, 0] = first[rows, :RHS]
        out[c, 1, :, :LANES] = second[rows]
        out[c, 1, :, LANES:] = tail[rows]


def local(kernel, ins, shapes, name, scratch=(), limit=24):
    return pl.pallas_call(
        kernel,
        in_specs=ins,
        out_specs=[VMEM] * len(shapes),
        out_shape=[jax.ShapeDtypeStruct(s, F32) for s in shapes],
        scratch_shapes=scratch,
        compiler_params=pltpu.CompilerParams(vmem_limit_bytes=limit * 2**20),
        name=name,
    )


SAME_CORE = [[2 * q + c for q in range(CHIPS)] for c in range(2)]
OTHER_CORE = [(i, i ^ 1) for i in range(ROWS)]


def exchange(x, axis, groups=None):
    return lax.all_to_all(x, axis, 0, 0, axis_index_groups=groups, tiled=True)


def on_device(gradient_rhs, pivots, solved_prev, upper_cols, upper_coupling, block_inverse):
    copies = pl.pallas_call(
        prepare_kernel,
        in_specs=[HBM] * 2,
        out_specs=HBM,
        out_shape=jax.ShapeDtypeStruct((CHIPS, 4, RW, CW), F32),
        scratch_shapes=[
            pltpu.VMEM((4, RW, CW), F32),
            pltpu.SemaphoreType.DMA((2,)),
            pltpu.SemaphoreType.DMA((CHIPS,)),
        ],
        compiler_params=pltpu.CompilerParams(vmem_limit_bytes=56 * 2**20),
        cost_estimate=pl.CostEstimate(flops=10**10, bytes_accessed=2**25, transcendentals=0),
        name="prepare",
    )(block_inverse, upper_coupling)
    own = exchange(copies, "row", SAME_CORE)

    mine, theirs = column_terms(
        jnp.swapaxes(solved_prev, 1, 2),
        upper_cols.reshape(2, -1, CW),
        gradient_rhs,
        pivots.reshape(2 * COLS, CW),
    )
    terms = mine + lax.ppermute(theirs, "row", OTHER_CORE)
    own, terms = lax.optimization_barrier((own, terms))
    other = lax.ppermute(own, "row", OTHER_CORE)
    terms = exchange(terms, "row", SAME_CORE)
    copies, rhs_second = local(
        first_kernel, [VMEM] * 3, [(COLS, 2 * RC, NB), (2 * RC, CW)], "first_share"
    )(terms, own, other)
    shares = exchange(copies, "col")
    (packed,) = local(
        coupling_kernel, [VMEM] * 4, [(CHIPS, 3 * RC, CW)], "coupling"
    )(shares, rhs_second, own, other)
    mine = exchange(packed, "row", SAME_CORE)
    theirs = lax.ppermute(mine, "row", OTHER_CORE)
    first, copies = local(
        second_kernel, [VMEM] * 3, [(2 * RW, ROWS * RC), (COLS, 2 * RW + 8 * (GROUPS - 1), LANES)], "second_share"
    )(mine, theirs, block_inverse)
    shares = exchange(copies, "col")
    (solved,) = local(join_kernel, [VMEM] * 2, [(2, 2, RW, RHS)], "join")(first, shares)
    return solved


def solution(mesh):
    placed = (
        P(None, "row", None),
        P(),
        P(None, "row", None),
        P(None, "row", None, "col"),
        P(None, "row", "col"),
        P(None, None, "row", "col"),
    )
    return jax.shard_map(
        on_device, mesh=mesh, in_specs=placed, out_specs=P(None, None, "row", None), check_vma=False
    )
```
